32 devices in a mesh: req: 4 (over y, x), exp: 8 (over z, core).
Axes of the slice: x: 2, y: 2, z: 4, core: 2. Of those that a mesh axis runs over, the one named last changes fastest.
Arguments:
- hidden: bfloat16 [8, 512, 2048], P('req', 'exp'), may hold values from -6 to 6
- q_new: bfloat16 [8, 16, 512, 128], P('req', None, 'exp'), may hold values from -480 to 480
- k_new: bfloat16 [8, 16, 512, 128], P('req', None, 'exp'), may hold values from -6 to 6
- v_new: bfloat16 [8, 16, 512, 128], P('req', None, 'exp'), may hold values from -6 to 6
- routes: int32 [8, 512, 6], P('req', 'exp'), may hold values from 0 to 63, all different within a row; in each aligned block of 64 rows (0 to 63, 64 to 127, ..., all dimensions but the last counted through in order) at most 8 rows name the same one
- slot_request: int32 [8], replicated, may hold values from 0 to 7, each once
- lengths: int32 [8], replicated, may hold values from 5 to 16384, as said below
- cycle_cache: bfloat16 [128, 2, 4096, 128], P(('req', 'exp')), may hold values from -6 to 6
- sink_cache: bfloat16 [128, 2, 4, 128], P(('req', 'exp')), may hold values from -6 to 6
- w_out: bfloat16 [2048, 2048], replicated, may hold values from -0.125 to 0.125
- norm_gain: float32 [2048], replicated, may hold values from 0.5 to 1.5
- router: bfloat16 [2048, 64], replicated, may hold values from -0.125 to 0.125
- w_gate: bfloat16 [2048, 90112], P(None, ('req', 'exp')), may hold values from -0.125 to 0.125
- w_up: bfloat16 [2048, 90112], P(None, ('req', 'exp')), may hold values from -0.125 to 0.125
- w_down: bfloat16 [90112, 2048], P(('req', 'exp')), may hold values from -0.15625 to 0.15625
Outputs:
- layer_out: bfloat16 [8, 512, 2048], P('req', 'exp')
- cycle_out: bfloat16 [128, 2, 4096, 128], P(('req', 'exp'))
The draws below stay inside these ranges and needn't reach their ends.
Inputs may be any that keep to these rules, and one draw needn't show every extreme that they name: In every aligned block of 64 rows of routes (the rows of one request on one index of exp) no expert is named by more than 8 rows, a bound that some block reaches. `slot_request`: each request once. `lengths`: some slot has exactly 16384 cached tokens, and some other fewer than 2048.
All inputs are finite; a program needn't handle non-finite values.
Results may differ from the reference program's by a relative error of at most 0.014.
The reference program's roundings to bfloat16 on the way count: a program that leaves them out, or rounds other values in their place, can miss the bound.
Values may be sent and summed in bfloat16 or wider, within the bound.
A program may use at most 192 MiB of HBM per device.

```python
import math
import jax
import jax.numpy as jnp
import numpy as np
from jax import lax

D = 2048
HEADS = 16
HD = 128
EXPERTS = 64
FF = 1408
TOP = 6
QD = 64
WINDOW = 4096
SINKS = 4
CTX = 16384
SPLIT = 2
QLEN = 512
REQS = 8
MOST = 8
N_EXP = 8


def draw_q_new(key, part):
    normal_key = jax.random.fold_in(key, 0)
    values = 2.0 * jnp.clip(jax.random.normal(normal_key, (REQS, HEADS, QLEN, HD), jnp.float32), -6.0, 6.0)
    return values.astype(jnp.bfloat16)


def draw_lengths(key, part):
    key_list = jax.random.split(key, 4)
    values = jax.random.randint(key_list[0], (REQS,), SINKS + 1, CTX + 1)
    longest = jax.random.randint(key_list[1], (), 0, REQS)
    shorter = (longest + 1 + jax.random.randint(key_list[2], (), 0, REQS - 1)) % REQS
    briefest = jax.random.randint(key_list[3], (), SINKS + 1, WINDOW // 2)
    places = jnp.arange(REQS)
    values = jnp.where(places == longest, CTX, values)
    values = jnp.where(places == shorter, briefest, values)
    return values.astype(jnp.int32)


def block_levels(stream_key, extent, cuts, least, largest):
    def one(position, parts):
        draws = jax.random.uniform(jax.random.fold_in(jax.random.fold_in(stream_key, 6), position), (parts,), jnp.float32, least / len(cuts), largest / len(cuts))
        return jnp.repeat(jnp.exp(draws), extent[position] // parts).reshape((-1,) + (1,) * (len(extent) - position - 1))

    gain = one(*cuts[0])
    for cut in cuts[1:]:
        gain = gain * one(*cut)
    return gain


def assign_block(own_key, own, number, rows, count, top, reach, slope):
    ranking = jax.random.permutation(own_key, count)
    crowded, ordinary = shares(count, rows * top, reach, slope, True), shares(count, rows * top, reach, slope, False)
    places = jnp.arange(count)

    def named(tallies, turn):
        used = int((tallies > 0).sum())
        fixed = max(1, used // 4)
        passed = fixed + (places - fixed + turn * (used - fixed)) % max(1, count - fixed)
        return jnp.zeros((count,), jnp.int32).at[ranking[jnp.where(places < fixed, places, passed)]].set(jnp.asarray(tallies, jnp.int32))

    tallies = jnp.where(number % 4 == 0, named(crowded, number // 4), named(ordinary, number - number // 4 - 1))
    mixed = jax.random.permutation(jax.random.fold_in(own, 3), count)
    giver, receiver = mixed[0:count // 2 * 2:2], mixed[1:count // 2 * 2:2]
    margin = jnp.minimum(tallies[giver] - 1, reach - tallies[receiver]) // 2
    margin = jnp.where((giver == ranking[0]) | (receiver == ranking[0]) | (tallies[receiver] == 0), 0, jnp.maximum(margin, 0))
    passed = jax.random.randint(jax.random.fold_in(own, 4), (count // 2,), 0, 1 << 20) % (margin + 1)
    tallies = tallies.at[giver].add(-passed).at[receiver].add(passed)
    items = jnp.searchsorted(jnp.cumsum(tallies), jnp.arange(rows * top), side="right").astype(jnp.int32)
    listing = items.reshape(top, rows).T
    listing = listing[jax.random.permutation(jax.random.fold_in(own, 1), rows)]
    turn = jax.random.randint(jax.random.fold_in(own, 2), (rows, 1), 0, top)
    return jnp.take_along_axis(listing, (jnp.arange(top)[None, :] + turn) % top, axis=1)


def shares(number_of, total, reach, skew, full):
    loads = [(1 << 20) // math.isqrt(rank ** skew) + 1 for rank in range(1, number_of + 1)]
    largest = reach if full else min(reach, max(-(-total // number_of), total * loads[0] // sum(loads)))
    least = 1 if total - largest >= number_of - 1 else 0
    counts, spare = [largest] + [least] * (number_of - 1), total - largest - least * (number_of - 1)
    while spare > 0:
        free = [i for i in range(1, number_of) if counts[i] < largest] or [i for i in range(1, number_of) if counts[i] < reach]
        mass, left = sum([loads[i] for i in free]), spare
        for i in free:
            addition = min(reach - counts[i], max(1, left * loads[i] // mass), spare)
            counts[i] = counts[i] + addition
            spare = spare - addition
    return np.array(counts)


def scatter_about(key, dims, deviation, limit, cuts=(), kind=jnp.bfloat16):
    result = deviation * jax.random.normal(key, dims, jnp.float32)
    if cuts:
        result = result * block_levels(key, dims, cuts, -0.22, 0.18)
    return jnp.clip(result, -limit, limit).astype(kind)


def setup_inputs(seed: int = 0) -> dict:
    splits = jax.random.split(jax.random.key(seed), 16)
    hidden = scatter_about(splits[0], (REQS, QLEN, D), 1.0, 6.0, ((0, 4), (1, 8)))
    q_new = draw_q_new(jax.random.fold_in(splits[15], 71), 0)
    k_new = scatter_about(splits[2], (REQS, HEADS, QLEN, HD), 1.0, 6.0, ((0, 4), (2, 8)))
    v_new = scatter_about(splits[3], (REQS, HEADS, QLEN, HD), 1.0, 6.0, ((0, 4), (2, 8)))
    routes_keys = jax.random.split(jax.random.fold_in(splits[4], 1), REQS * QLEN // QD)
    routes_turns = jax.random.permutation(jax.random.fold_in(splits[4], 3), REQS * QLEN // QD)
    routes = jax.vmap(lambda own, number: assign_block(jax.random.fold_in(splits[4], 2), own, number, QD, EXPERTS, TOP, MOST, 2))(routes_keys, routes_turns).reshape((REQS, QLEN, TOP))
    slot_request = jax.random.permutation(splits[5], REQS).astype(jnp.int32)
    lengths = draw_lengths(jax.random.fold_in(splits[15], 71), 0)
    cycle_cache = scatter_about(splits[7], (REQS * HEADS, 2, WINDOW, HD), 1.0, 6.0, ((0, 32),))
    sink_cache = scatter_about(splits[8], (REQS * HEADS, 2, SINKS, HD), 1.0, 6.0, ((0, 32),))
    w_out = scatter_about(splits[9], (D, D), D ** -0.5, 0.125)
    norm_gain = jnp.clip(1.0 + 0.1 * jax.random.normal(splits[10], (D,), jnp.float32), 0.5, 1.5)
    router = scatter_about(splits[11], (D, EXPERTS), D ** -0.5, 0.125)
    w_gate = scatter_about(splits[12], (D, EXPERTS * FF), D ** -0.5, 0.125, ((1, 32),))
    w_up = scatter_about(splits[13], (D, EXPERTS * FF), D ** -0.5, 0.125, ((1, 32),))
    w_down = scatter_about(splits[14], (EXPERTS * FF, D), FF ** -0.5, 0.15625, ((0, 32),))
    return dict(hidden=hidden, q_new=q_new, k_new=k_new, v_new=v_new, routes=routes, slot_request=slot_request, lengths=lengths, cycle_cache=cycle_cache, sink_cache=sink_cache, w_out=w_out, norm_gain=norm_gain, router=router, w_gate=w_gate, w_up=w_up, w_down=w_down)


def rotate(vectors, positions):
    half_width = vectors.shape[-1] // 2
    frequency = 10000.0 ** (-2.0 * jnp.arange(half_width, dtype=jnp.float32) / vectors.shape[-1])
    angles = positions.astype(jnp.float32)[:, None] * frequency[None, :]
    cosine = jnp.cos(angles)
    sine_part = jnp.sin(angles)
    low_half = vectors[..., :half_width]
    high_half = vectors[..., half_width:]
    return jnp.concatenate([low_half * cosine - high_half * sine_part, high_half * cosine + low_half * sine_part], axis=-1)

def attend_pair(query_rows, key_new, value_new, cycle_pair, sink_pair, length):
    positions = length + jnp.arange(QLEN, dtype=jnp.int32)
    q_rot = rotate(query_rows.astype(jnp.float32), positions).astype(jnp.bfloat16)
    k_rot = rotate(key_new.astype(jnp.float32), positions).astype(jnp.bfloat16)
    cycle_slots = jnp.arange(WINDOW, dtype=jnp.int32)
    cycle_positions = cycle_slots + WINDOW * ((length - 1 - cycle_slots) // WINDOW)
    key_rows = jnp.concatenate([cycle_pair[0], k_rot], 0)
    value_rows = jnp.concatenate([cycle_pair[1], value_new], 0)
    key_positions = jnp.concatenate([cycle_positions, positions], 0)
    visible = (key_positions[None, :] >= 0) & (key_positions[None, :] <= positions[:, None]) & (key_positions[None, :] > positions[:, None] - WINDOW)
    score_scale = HD ** (-0.5)
    scores = jnp.dot(q_rot, key_rows.T, preferred_element_type=jnp.float32) * score_scale
    scores = jnp.where(visible, scores, -jnp.inf)
    sink_scores = jnp.dot(q_rot, sink_pair[0].T, preferred_element_type=jnp.float32) * score_scale
    sink_visible = jnp.arange(SINKS, dtype=jnp.int32)[None, :] <= positions[:, None] - WINDOW
    sink_scores = jnp.where(sink_visible, sink_scores, -jnp.inf)
    highest = jnp.maximum(lax.optimization_barrier(jnp.max(scores, axis=1)), lax.optimization_barrier(jnp.max(sink_scores, axis=1)))[:, None]
    weights = jnp.exp(scores - highest)
    sink_weights = jnp.exp(sink_scores - highest)
    denominator = lax.optimization_barrier(jnp.sum(weights, axis=1)) + lax.optimization_barrier(jnp.sum(sink_weights, axis=1))
    blended = jnp.dot(weights.astype(jnp.bfloat16), value_rows, preferred_element_type=jnp.float32)
    blended = blended + jnp.dot(sink_weights.astype(jnp.bfloat16), sink_pair[1], preferred_element_type=jnp.float32)
    context = (blended / denominator[:, None]).astype(jnp.bfloat16)
    new_slots = positions % WINDOW
    updated = jnp.stack([cycle_pair[0].at[new_slots].set(k_rot), cycle_pair[1].at[new_slots].set(value_new)])
    return (context, updated)

def reference(hidden, q_new, k_new, v_new, routes, slot_request, lengths, cycle_cache, sink_cache, w_out, norm_gain, router, w_gate, w_up, w_down):
    pair_count = REQS * HEADS
    query_all = jnp.take(q_new, slot_request, axis=0).reshape(pair_count, QLEN, HD)
    key_all = jnp.take(k_new, slot_request, axis=0).reshape(pair_count, QLEN, HD)
    value_all = jnp.take(v_new, slot_request, axis=0).reshape(pair_count, QLEN, HD)
    pair_lengths = jnp.repeat(lengths, HEADS)
    context, cycle_out = lax.map(lambda packed: attend_pair(*packed), (query_all, key_all, value_all, cycle_cache, sink_cache, pair_lengths))
    context = context.reshape(REQS, HEADS, QLEN, HD)
    projected = jnp.einsum('shqd,hde->sqe', context.astype(jnp.float32), w_out.reshape(HEADS, HD, D).astype(jnp.float32))
    residual = jnp.take(hidden, slot_request, axis=0).astype(jnp.float32) + projected
    inverse = lax.rsqrt(lax.optimization_barrier(jnp.mean(residual * residual, axis=-1, keepdims=True)) + 1e-06)
    normed = (residual * inverse * norm_gain.astype(jnp.float32)).astype(jnp.bfloat16).reshape(REQS * QLEN, D)
    logits = jnp.dot(normed, router, preferred_element_type=jnp.float32)
    chosen = jnp.take(routes, slot_request, axis=0).reshape(REQS * QLEN, TOP)
    gates = jax.nn.softmax(jnp.take_along_axis(logits, chosen, axis=1), axis=-1)
    capacity = REQS * N_EXP * MOST
    half_units = FF // SPLIT

    def per_expert(running, expert):
        matched = chosen == expert
        member = jnp.any(matched, axis=1)
        weight_row = lax.optimization_barrier(jnp.sum(jnp.where(matched, gates, 0.0), axis=1))
        indices = jnp.nonzero(member, size=capacity, fill_value=0)[0].astype(jnp.int32)
        filled = jnp.arange(capacity, dtype=jnp.int32) < jnp.sum(member.astype(jnp.int32))
        selected = jnp.take(normed, indices, axis=0)
        gate_cols = lax.dynamic_slice_in_dim(w_gate, expert * FF, FF, 1)
        up_cols = lax.dynamic_slice_in_dim(w_up, expert * FF, FF, 1)
        down_rows = lax.dynamic_slice_in_dim(w_down, expert * FF, FF, 0)
        summed = jnp.zeros((capacity, D), jnp.float32)
        for piece_number in range(SPLIT):
            first_unit = piece_number * half_units
            gate_part = jnp.dot(selected, gate_cols[:, first_unit:first_unit + half_units], preferred_element_type=jnp.float32)
            up_part = jnp.dot(selected, up_cols[:, first_unit:first_unit + half_units], preferred_element_type=jnp.float32)
            active = (jax.nn.silu(gate_part) * up_part).astype(jnp.bfloat16)
            output_part = jnp.dot(active, down_rows[first_unit:first_unit + half_units], preferred_element_type=jnp.float32).astype(jnp.bfloat16)
            summed = summed + lax.optimization_barrier(output_part).astype(jnp.float32)
        scaled = jnp.where(filled, jnp.take(weight_row, indices), 0.0)[:, None] * summed
        return (running.at[indices].add(scaled), None)
    moe, _ = lax.scan(per_expert, jnp.zeros((REQS * QLEN, D), jnp.float32), jnp.arange(EXPERTS, dtype=jnp.int32))
    layer_out = (residual.reshape(REQS * QLEN, D) + moe).astype(jnp.bfloat16).reshape(REQS, QLEN, D)
    return (layer_out, cycle_out)
```

```python
import functools

import jax
import jax.numpy as jnp
from jax import lax
from jax.experimental import pallas as pl
from jax.experimental.pallas import tpu as pltpu
from jax.sharding import PartitionSpec as P

SPLIT = 2
SINK_PAD = 128
ALIGN = 32
LOG2E = 1.4426950408889634


def angle_tables(length, seq_len, head_dim):
    half_width = head_dim // 2
    positions = length + jnp.arange(seq_len, dtype=jnp.int32)
    frequency = 10000.0 ** (-2.0 * jnp.arange(half_width, dtype=jnp.float32) / head_dim)
    angles = positions.astype(jnp.float32)[:, None] * frequency[None, :]
    cosine = jnp.cos(angles)
    sine = jnp.sin(angles)
    return (
        jnp.concatenate([cosine, cosine], axis=-1),
        jnp.concatenate([-sine, sine], axis=-1),
    )


def attend_kernel(
    sinks,
    tile_keys,
    tile_rows,
    length_ref,
    fresh_ref,
    cycle_ref,
    sink_ref,
    cosine_ref,
    sine_ref,
    context_ref,
    updated_ref,
    query,
    extra_key,
    extra_value,
    stage,
    blend,
    highest,
):
    seq_len, head_dim = query.shape
    window = cycle_ref.shape[2]
    length = length_ref[0]
    offset = lax.rem(length, window)
    factor = head_dim ** (-0.5) * LOG2E

    def turned(index):
        rows = fresh_ref[:, index, 0].reshape(seq_len, head_dim).astype(jnp.float32)
        return rows * cosine_ref[...] + pltpu.roll(rows, head_dim // 2, 1) * sine_ref[...]

    query[...] = turned(0).astype(jnp.bfloat16)
    key_turned = turned(1)
    value_rows = fresh_ref[:, 2, 0].reshape(seq_len, head_dim)
    stage[0, ALIGN : ALIGN + seq_len] = key_turned
    stage[1, ALIGN : ALIGN + seq_len] = value_rows.astype(jnp.float32)
    extra_key[:seq_len] = key_turned.astype(jnp.bfloat16)
    extra_value[:seq_len] = value_rows
    extra_key[seq_len:] = sink_ref[0, 0]
    extra_value[seq_len:] = sink_ref[0, 1]

    def blended(weights, values):
        wide = jnp.concatenate([values, jnp.ones_like(values)], axis=1)
        return jnp.dot(weights.astype(jnp.bfloat16), wide, preferred_element_type=jnp.float32)

    def dots(rows, keys):
        return lax.dot_general(
            rows, keys, (((1,), (1,)), ((), ())), preferred_element_type=jnp.float32
        )

    def first(block, carry):
        start = pl.multiple_of(block * tile_rows, tile_rows)
        here = pl.ds(start, tile_rows)
        scores = dots(query[here, :], extra_key[...])
        width = seq_len + SINK_PAD
        row = start + lax.broadcasted_iota(jnp.int32, (tile_rows, 1), 0)
        column = lax.broadcasted_iota(jnp.int32, (1, width), 1)
        sink_limit = jnp.minimum(length + row - window, sinks - 1) + seq_len
        is_new = column < seq_len
        new_key = jnp.where(is_new, column, window)
        sink_key = jnp.where(is_new, 2 * window + seq_len, column)
        seen = (new_key <= row) | (sink_key <= sink_limit)
        scores = jnp.where(seen, scores, -jnp.inf)
        top = jnp.max(scores, axis=1, keepdims=True)
        weights = jnp.exp2((scores - top) * factor)
        blend[here, :] = blended(weights, extra_value[...])
        highest[here, :] = jnp.broadcast_to(top, (tile_rows, head_dim))
        return carry

    lax.fori_loop(0, seq_len // tile_rows, first, 0)

    def tile(number, carry):
        slot_start = pl.multiple_of(number * tile_keys, tile_keys)
        keys_here = pl.ds(slot_start, tile_keys)
        age_start = lax.rem(slot_start - offset + window, window)
        partial = (age_start < seq_len) | (age_start + tile_keys > window) | (length < window)

        def rows_step(masked, start):
            here = pl.ds(start, tile_rows)
            scores = dots(query[here, :], cycle_ref[0, 0, keys_here, :])
            if masked:
                row = start + lax.broadcasted_iota(jnp.int32, (tile_rows, 1), 0)
                column = lax.broadcasted_iota(jnp.int32, (1, tile_keys), 1)
                age = column + age_start
                age = jnp.where(age >= window, age - window, age)
                scores = jnp.where(age >= jnp.maximum(row + 1, window - length), scores, -jnp.inf)
            before = highest[here, :]
            top = jnp.maximum(before[:, :1], jnp.max(scores, axis=1, keepdims=True))
            weights = jnp.exp2((scores - top) * factor)
            keep = jnp.exp2((before[:, :1] - top) * factor)
            blend[here, :] = blend[here, :] * keep + blended(
                weights, cycle_ref[0, 1, keys_here, :]
            )
            highest[here, :] = jnp.broadcast_to(top, (tile_rows, head_dim))

        def all_rows(masked):
            pairs = 2 if (seq_len // tile_rows) % 2 == 0 else 1

            def body(step, inner):
                for part in range(pairs):
                    start = pl.multiple_of((step * pairs + part) * tile_rows, tile_rows)
                    rows_step(masked, start)
                return inner

            lax.fori_loop(0, seq_len // tile_rows // pairs, body, 0)

        live = slot_start < length

        @pl.when(live & partial)
        def _():
            all_rows(True)

        @pl.when(live & jnp.logical_not(partial))
        def _():
            all_rows(False)

        return carry

    lax.fori_loop(0, window // tile_keys, tile, 0)

    total = blend[:, head_dim:]
    context = (blend[:, :head_dim] / total).astype(jnp.bfloat16)
    context_ref[:, 0] = context.reshape(context_ref.shape[0], context_ref.shape[2], head_dim)

    updated_ref[...] = cycle_ref[...]
    base = lax.div(offset, ALIGN) * ALIGN
    shift = offset - base

    def put(chunk, carry):
        at = pl.multiple_of(lax.rem(base + chunk * ALIGN, window), ALIGN)
        fresh_row = (
            chunk * ALIGN - shift + lax.broadcasted_iota(jnp.int32, (ALIGN, head_dim), 0)
        )
        inside = (fresh_row >= 0) & (fresh_row < seq_len)
        for which in range(2):
            fresh = stage[which, pl.ds(ALIGN + chunk * ALIGN - shift, ALIGN), :]
            old = updated_ref[0, which, pl.ds(at, ALIGN), :].astype(jnp.float32)
            updated_ref[0, which, pl.ds(at, ALIGN), :] = jnp.where(inside, fresh, old).astype(
                jnp.bfloat16
            )
        return carry

    lax.fori_loop(0, seq_len // ALIGN + 1, put, 0)


def attend(fresh, cycle_cache, sink_cache, length):
    members, _, pairs, local_rows, head_dim = fresh.shape
    seq_len = members * local_rows
    window = cycle_cache.shape[2]
    sinks = sink_cache.shape[2]
    tile_keys = min(1024, window)
    tile_rows = min(256, seq_len)
    cosine, sine = angle_tables(length, seq_len, head_dim)
    sink_wide = jnp.pad(sink_cache, ((0, 0), (0, 0), (0, SINK_PAD - sinks), (0, 0)))
    return pl.pallas_call(
        functools.partial(attend_kernel, sinks, tile_keys, tile_rows),
        out_shape=(
            jax.ShapeDtypeStruct((members, pairs, local_rows, head_dim), jnp.bfloat16),
            jax.ShapeDtypeStruct(cycle_cache.shape, cycle_cache.dtype),
        ),
        grid_spec=pltpu.PrefetchScalarGridSpec(
            num_scalar_prefetch=1,
            grid=(pairs,),
            in_specs=[
                pl.BlockSpec((members, 3, 1, local_rows, head_dim), lambda p, _: (0, 0, p, 0, 0)),
                pl.BlockSpec((1, 2, window, head_dim), lambda p, _: (p, 0, 0, 0)),
                pl.BlockSpec((1, 2, SINK_PAD, head_dim), lambda p, _: (p, 0, 0, 0)),
                pl.BlockSpec((seq_len, head_dim), lambda p, _: (0, 0)),
                pl.BlockSpec((seq_len, head_dim), lambda p, _: (0, 0)),
            ],
            out_specs=[
                pl.BlockSpec((members, 1, local_rows, head_dim), lambda p, _: (0, p, 0, 0)),
                pl.BlockSpec((1, 2, window, head_dim), lambda p, _: (p, 0, 0, 0)),
            ],
            scratch_shapes=[
                pltpu.VMEM((seq_len, head_dim), jnp.bfloat16),
                pltpu.VMEM((seq_len + SINK_PAD, head_dim), jnp.bfloat16),
                pltpu.VMEM((seq_len + SINK_PAD, head_dim), jnp.bfloat16),
                pltpu.VMEM((2, seq_len + 2 * ALIGN, head_dim), jnp.float32),
                pltpu.VMEM((seq_len, 2 * head_dim), jnp.float32),
                pltpu.VMEM((seq_len, head_dim), jnp.float32),
            ],
        ),
        compiler_params=pltpu.CompilerParams(vmem_limit_bytes=48 * 1024 * 1024),
        cost_estimate=pl.CostEstimate(
            flops=4 * pairs * seq_len * (window + seq_len) * head_dim,
            bytes_accessed=4 * cycle_cache.size,
            transcendentals=pairs * seq_len * (window + seq_len),
        ),
    )(length.reshape(1), fresh, cycle_cache, sink_wide, cosine, sine)


def on_device(
    hidden,
    q_new,
    k_new,
    v_new,
    routes,
    slot_request,
    lengths,
    cycle_cache,
    sink_cache,
    w_out,
    norm_gain,
    router,
    w_gate,
    w_up,
    w_down,
):
    group_width = lax.axis_size("exp")
    group_count = lax.axis_size("req")
    devices_all = group_count * group_width
    group_index = lax.axis_index("req")
    member_index = lax.axis_index("exp")
    slots_here, local_rows, model_width = hidden.shape
    head_count = q_new.shape[1]
    head_dim = q_new.shape[3]
    experts_all = router.shape[1]
    pair_count = slots_here * head_count
    pairs_here = pair_count // group_width
    members_of_slot = head_count // pairs_here

    requests = lax.dynamic_slice_in_dim(slot_request, group_index * slots_here, slots_here)
    fresh_all = lax.all_gather(jnp.stack([q_new, k_new, v_new], 1), "req", axis=0, tiled=True)
    fresh_sel = jnp.take(fresh_all, requests, axis=0)
    fresh_out = (
        fresh_sel.reshape(
            slots_here, 3, members_of_slot, pairs_here, local_rows, head_dim
        )
        .transpose(0, 2, 1, 3, 4, 5)
        .reshape(group_width, 3, pairs_here, local_rows, head_dim)
    )
    fresh = lax.all_to_all(fresh_out, "exp", split_axis=0, concat_axis=0, tiled=True)
    slot_here = group_index * slots_here + member_index // members_of_slot
    length = lax.dynamic_index_in_dim(lengths, slot_here, keepdims=False)

    hidden_sel = jnp.take(lax.all_gather(hidden, "req", axis=0, tiled=True), requests, axis=0)
    route_sel = jnp.take(lax.all_gather(routes, "req", axis=0, tiled=True), requests, axis=0)
    route_group = lax.all_gather(route_sel, "exp", axis=0)

    context, cycle_out = attend(fresh, cycle_cache, sink_cache, length)
    context_rows = lax.all_to_all(context, "exp", split_axis=0, concat_axis=0, tiled=True)
    context_rows = context_rows.reshape(slots_here, head_count, local_rows, head_dim)
    projected = jnp.einsum(
        "shqd,hde->sqe",
        context_rows,
        w_out.reshape(head_count, head_dim, model_width),
        preferred_element_type=jnp.float32,
    )
    residual = hidden_sel.astype(jnp.float32) + projected
    inverse = lax.rsqrt(jnp.mean(residual * residual, axis=-1, keepdims=True) + 1e-06)
    normed = (residual * inverse * norm_gain).astype(jnp.bfloat16)

    blocks = group_width * slots_here
    most_slots = max(2, local_rows // 8)
    sub_here = experts_all * SPLIT // devices_all
    units = max(1, sub_here // SPLIT)
    pieces = max(1, SPLIT // sub_here)
    owners = jnp.arange(group_count, dtype=jnp.int32) * group_width + member_index
    served = (
        owners[:, None] * units + jnp.arange(units, dtype=jnp.int32)[None, :]
    ).reshape(-1) // pieces
    served_count = group_count * units
    route_blocks = route_group.reshape(blocks, local_rows, -1)
    named = jnp.any(route_blocks[..., None] == served, axis=2)
    earlier_rows = jnp.arange(local_rows)[:, None] > jnp.arange(local_rows)[None, :]
    earlier = jnp.einsum(
        "qp,bpe->bqe",
        earlier_rows.astype(jnp.bfloat16),
        named.astype(jnp.bfloat16),
        preferred_element_type=jnp.float32,
    ).astype(jnp.int32)
    chosen = named[..., None] & (
        earlier[..., None] == jnp.arange(most_slots, dtype=jnp.int32)
    )

    rows_group = lax.all_gather(normed, "exp", axis=0).reshape(blocks, local_rows, model_width)
    outgoing = jnp.einsum(
        "bqer,bqd->ebrd",
        chosen.astype(jnp.bfloat16),
        rows_group,
        preferred_element_type=jnp.float32,
    ).astype(jnp.bfloat16)
    landed = lax.all_to_all(
        outgoing.reshape(group_count, units, blocks * most_slots, model_width),
        "req",
        split_axis=0,
        concat_axis=0,
        tiled=True,
    )
    logits = jnp.einsum("bqd,de->bqe", rows_group, router, preferred_element_type=jnp.float32)
    routed = jnp.any(
        route_blocks[..., None] == jnp.arange(experts_all, dtype=jnp.int32), axis=2
    )
    logits = jnp.where(routed, logits, -jnp.inf)
    gates_all = jax.nn.softmax(logits, axis=-1)
    gates = jnp.take(gates_all, served, axis=2)
    weights = jnp.where(chosen, gates[..., None], 0.0)
    weights_high = lax.reduce_precision(weights, 8, 7)
    weights_low = (weights - weights_high).astype(jnp.bfloat16)
    weights_high = weights_high.astype(jnp.bfloat16)

    hidden_units = w_gate.shape[1] // units
    replies = []
    for unit in range(units):
        rows = landed[:, unit].reshape(group_count * blocks * most_slots, model_width)
        span = slice(unit * hidden_units, (unit + 1) * hidden_units)
        gate_part = jnp.dot(rows, w_gate[:, span], preferred_element_type=jnp.float32)
        up_part = jnp.dot(rows, w_up[:, span], preferred_element_type=jnp.float32)
        active = (jax.nn.silu(gate_part) * up_part).astype(jnp.bfloat16)
        reply = jnp.dot(active, w_down[span], preferred_element_type=jnp.float32)
        replies.append(
            reply.astype(jnp.bfloat16).reshape(
                group_count, 1, blocks * most_slots, model_width
            )
        )
    reply = replies[0] if units == 1 else jnp.concatenate(replies, 1)
    returned = lax.all_to_all(reply, "req", split_axis=0, concat_axis=0, tiled=True).reshape(
        served_count, blocks, most_slots, model_width
    )

    def combined(part):
        return jnp.einsum("bqer,ebrd->bqd", part, returned, preferred_element_type=jnp.float32)

    partial = (combined(weights_high) + combined(weights_low)).astype(jnp.bfloat16)
    moe = lax.psum_scatter(
        partial.reshape(group_width, slots_here, local_rows, model_width),
        "exp",
        scatter_dimension=0,
        tiled=False,
    )
    layer_out = (residual + moe.astype(jnp.float32)).astype(jnp.bfloat16)
    return (layer_out, cycle_out)


def solution(mesh):
    in_specs = (
        P("req", "exp", None),
        P("req", None, "exp", None),
        P("req", None, "exp", None),
        P("req", None, "exp", None),
        P("req", "exp", None),
        P(),
        P(),
        P(("req", "exp"), None, None, None),
        P(("req", "exp"), None, None, None),
        P(),
        P(),
        P(),
        P(None, ("req", "exp")),
        P(None, ("req", "exp")),
        P(("req", "exp"), None),
    )
    out_specs = (P("req", "exp", None), P(("req", "exp"), None, None, None))
    return jax.shard_map(
        on_device, mesh=mesh, in_specs=in_specs, out_specs=out_specs, check_vma=False
    )
```

```python
import functools
import itertools

import jax
import jax.numpy as jnp
from jax import lax
from jax.experimental import pallas as pl
from jax.experimental.pallas import tpu as pltpu
from jax.sharding import PartitionSpec as P

SPLIT = 2
SINK_PAD = 128
ALIGN = 32
LOG2E = 1.4426950408889634


def angle_tables(length, seq_len, head_dim):
    half_width = head_dim // 2
    positions = length + jnp.arange(seq_len, dtype=jnp.int32)
    frequency = 10000.0 ** (-2.0 * jnp.arange(half_width, dtype=jnp.float32) / head_dim)
    angles = positions.astype(jnp.float32)[:, None] * frequency[None, :]
    cosine = jnp.cos(angles)
    sine = jnp.sin(angles)
    return (
        jnp.concatenate([cosine, cosine], axis=-1),
        jnp.concatenate([-sine, sine], axis=-1),
    )


def attend_kernel(
    sinks,
    tile_keys,
    tile_rows,
    length_ref,
    fresh_ref,
    cycle_ref,
    sink_ref,
    cosine_ref,
    sine_ref,
    context_ref,
    updated_ref,
    query,
    extra_key,
    extra_value,
    stage,
    blend,
    highest,
):
    seq_len, head_dim = query.shape
    window = cycle_ref.shape[2]
    length = length_ref[0]
    offset = lax.rem(length, window)
    factor = head_dim ** (-0.5) * LOG2E

    def turned(index):
        rows = fresh_ref[:, index, 0].reshape(seq_len, head_dim).astype(jnp.float32)
        return rows * cosine_ref[...] + pltpu.roll(rows, head_dim // 2, 1) * sine_ref[...]

    query[...] = turned(0).astype(jnp.bfloat16)
    key_turned = turned(1)
    value_rows = fresh_ref[:, 2, 0].reshape(seq_len, head_dim)
    stage[0, ALIGN : ALIGN + seq_len] = key_turned
    stage[1, ALIGN : ALIGN + seq_len] = value_rows.astype(jnp.float32)
    extra_key[:seq_len] = key_turned.astype(jnp.bfloat16)
    extra_value[:seq_len] = value_rows
    extra_key[seq_len:] = sink_ref[0, 0]
    extra_value[seq_len:] = sink_ref[0, 1]

    def blended(weights, values):
        wide = jnp.concatenate([values, jnp.ones_like(values)], axis=1)
        return jnp.dot(weights.astype(jnp.bfloat16), wide, preferred_element_type=jnp.float32)

    def dots(rows, keys):
        return lax.dot_general(
            rows, keys, (((1,), (1,)), ((), ())), preferred_element_type=jnp.float32
        )

    def first(block, carry):
        start = pl.multiple_of(block * tile_rows, tile_rows)
        here = pl.ds(start, tile_rows)
        scores = dots(query[here, :], extra_key[...])
        width = seq_len + SINK_PAD
        row = start + lax.broadcasted_iota(jnp.int32, (tile_rows, 1), 0)
        column = lax.broadcasted_iota(jnp.int32, (1, width), 1)
        sink_limit = jnp.minimum(length + row - window, sinks - 1) + seq_len
        is_new = column < seq_len
        new_key = jnp.where(is_new, column, window)
        sink_key = jnp.where(is_new, 2 * window + seq_len, column)
        seen = (new_key <= row) | (sink_key <= sink_limit)
        scores = jnp.where(seen, scores, -jnp.inf)
        top = jnp.max(scores, axis=1, keepdims=True)
        weights = jnp.exp2((scores - top) * factor)
        blend[here, :] = blended(weights, extra_value[...])
        highest[here, :] = jnp.broadcast_to(top, (tile_rows, head_dim))
        return carry

    lax.fori_loop(0, seq_len // tile_rows, first, 0)

    def tile(number, carry):
        slot_start = pl.multiple_of(number * tile_keys, tile_keys)
        keys_here = pl.ds(slot_start, tile_keys)
        age_start = lax.rem(slot_start - offset + window, window)
        partial = (age_start < seq_len) | (age_start + tile_keys > window) | (length < window)

        def rows_step(masked, start):
            here = pl.ds(start, tile_rows)
            scores = dots(query[here, :], cycle_ref[0, 0, keys_here, :])
            if masked:
                row = start + lax.broadcasted_iota(jnp.int32, (tile_rows, 1), 0)
                column = lax.broadcasted_iota(jnp.int32, (1, tile_keys), 1)
                age = column + age_start
                age = jnp.where(age >= window, age - window, age)
                scores = jnp.where(age >= jnp.maximum(row + 1, window - length), scores, -jnp.inf)
            before = highest[here, :]
            top = jnp.maximum(before[:, :1], jnp.max(scores, axis=1, keepdims=True))
            weights = jnp.exp2((scores - top) * factor)
            keep = jnp.exp2((before[:, :1] - top) * factor)
            blend[here, :] = blend[here, :] * keep + blended(
                weights, cycle_ref[0, 1, keys_here, :]
            )
            highest[here, :] = jnp.broadcast_to(top, (tile_rows, head_dim))

        def all_rows(masked):
            pairs = 2 if (seq_len // tile_rows) % 2 == 0 else 1

            def body(step, inner):
                for part in range(pairs):
                    start = pl.multiple_of((step * pairs + part) * tile_rows, tile_rows)
                    rows_step(masked, start)
                return inner

            lax.fori_loop(0, seq_len // tile_rows // pairs, body, 0)

        live = slot_start < length

        @pl.when(live & partial)
        def _():
            all_rows(True)

        @pl.when(live & jnp.logical_not(partial))
        def _():
            all_rows(False)

        return carry

    lax.fori_loop(0, window // tile_keys, tile, 0)

    total = blend[:, head_dim:]
    context = (blend[:, :head_dim] / total).astype(jnp.bfloat16)
    context_ref[:, 0] = context.reshape(context_ref.shape[0], context_ref.shape[2], head_dim)

    updated_ref[...] = cycle_ref[...]
    base = lax.div(offset, ALIGN) * ALIGN
    shift = offset - base

    def put(chunk, carry):
        at = pl.multiple_of(lax.rem(base + chunk * ALIGN, window), ALIGN)
        fresh_row = (
            chunk * ALIGN - shift + lax.broadcasted_iota(jnp.int32, (ALIGN, head_dim), 0)
        )
        inside = (fresh_row >= 0) & (fresh_row < seq_len)
        for which in range(2):
            fresh = stage[which, pl.ds(ALIGN + chunk * ALIGN - shift, ALIGN), :]
            old = updated_ref[0, which, pl.ds(at, ALIGN), :].astype(jnp.float32)
            updated_ref[0, which, pl.ds(at, ALIGN), :] = jnp.where(inside, fresh, old).astype(
                jnp.bfloat16
            )
        return carry

    lax.fori_loop(0, seq_len // ALIGN + 1, put, 0)


def attend(fresh, cycle_cache, sink_cache, length):
    members, _, pairs, local_rows, head_dim = fresh.shape
    seq_len = members * local_rows
    window = cycle_cache.shape[2]
    sinks = sink_cache.shape[2]
    tile_keys = min(1024, window)
    tile_rows = min(256, seq_len)
    cosine, sine = angle_tables(length, seq_len, head_dim)
    sink_wide = jnp.pad(sink_cache, ((0, 0), (0, 0), (0, SINK_PAD - sinks), (0, 0)))
    return pl.pallas_call(
        functools.partial(attend_kernel, sinks, tile_keys, tile_rows),
        out_shape=(
            jax.ShapeDtypeStruct((members, pairs, local_rows, head_dim), jnp.bfloat16),
            jax.ShapeDtypeStruct(cycle_cache.shape, cycle_cache.dtype),
        ),
        grid_spec=pltpu.PrefetchScalarGridSpec(
            num_scalar_prefetch=1,
            grid=(pairs,),
            in_specs=[
                pl.BlockSpec((members, 3, 1, local_rows, head_dim), lambda p, _: (0, 0, p, 0, 0)),
                pl.BlockSpec((1, 2, window, head_dim), lambda p, _: (p, 0, 0, 0)),
                pl.BlockSpec((1, 2, SINK_PAD, head_dim), lambda p, _: (p, 0, 0, 0)),
                pl.BlockSpec((seq_len, head_dim), lambda p, _: (0, 0)),
                pl.BlockSpec((seq_len, head_dim), lambda p, _: (0, 0)),
            ],
            out_specs=[
                pl.BlockSpec((members, 1, local_rows, head_dim), lambda p, _: (0, p, 0, 0)),
                pl.BlockSpec((1, 2, window, head_dim), lambda p, _: (p, 0, 0, 0)),
            ],
            scratch_shapes=[
                pltpu.VMEM((seq_len, head_dim), jnp.bfloat16),
                pltpu.VMEM((seq_len + SINK_PAD, head_dim), jnp.bfloat16),
                pltpu.VMEM((seq_len + SINK_PAD, head_dim), jnp.bfloat16),
                pltpu.VMEM((2, seq_len + 2 * ALIGN, head_dim), jnp.float32),
                pltpu.VMEM((seq_len, 2 * head_dim), jnp.float32),
                pltpu.VMEM((seq_len, head_dim), jnp.float32),
            ],
        ),
        compiler_params=pltpu.CompilerParams(vmem_limit_bytes=48 * 1024 * 1024),
        cost_estimate=pl.CostEstimate(
            flops=4 * pairs * seq_len * (window + seq_len) * head_dim,
            bytes_accessed=4 * cycle_cache.size,
            transcendentals=pairs * seq_len * (window + seq_len),
        ),
    )(length.reshape(1), fresh, cycle_cache, sink_wide, cosine, sine)


def from_holders(held, slot_request, requests):
    slots_here = held.shape[0]
    group_count = lax.axis_size("req")
    if slots_here != 2 or group_count > 4:
        return jnp.take(lax.all_gather(held, "req", axis=0, tiled=True), requests, axis=0)
    group_index = lax.axis_index("req")
    slot_of = jnp.argsort(slot_request)
    flips = jnp.array(list(itertools.product(range(2), repeat=group_count)), jnp.int32)
    colours = (flips[:, :, None] ^ jnp.arange(2, dtype=jnp.int32)).reshape(-1, 2 * group_count)
    by_request = colours[:, slot_of].reshape(-1, group_count, 2)
    fits = jnp.all(by_request[..., 0] != by_request[..., 1], axis=1)
    pick = jnp.argmax(fits)
    flip = flips[pick]
    request_colour = by_request[pick]
    orders = list(itertools.permutations(range(group_count)))
    table = jnp.array(orders, jnp.int32)
    slot_groups = jnp.arange(group_count, dtype=jnp.int32)
    came = []
    for colour in range(2):
        source = slot_request[2 * slot_groups + (flip ^ colour)] // 2
        number = jnp.argmax(jnp.all(table == source, axis=1)).astype(jnp.int32)
        mine = request_colour[group_index, 1] == colour
        block = jnp.where(mine, held[1], held[0])

        def moved(order, payload):
            return lax.ppermute(payload, "req", [(order[g], g) for g in range(group_count)])

        branches = [functools.partial(moved, order) for order in orders]
        came.append(lax.switch(number, branches, block))
    swapped = flip[group_index] == 1
    return jnp.stack(
        [jnp.where(swapped, came[1], came[0]), jnp.where(swapped, came[0], came[1])]
    )


def swap_all(parts):
    count = lax.axis_size("req")
    return [parts[0]] + [
        lax.ppermute(parts[k], "req", [(g, g ^ k) for g in range(count)])
        for k in range(1, count)
    ]


def on_device(
    hidden,
    q_new,
    k_new,
    v_new,
    routes,
    slot_request,
    lengths,
    cycle_cache,
    sink_cache,
    w_out,
    norm_gain,
    router,
    w_gate,
    w_up,
    w_down,
):
    group_width = lax.axis_size("exp")
    group_count = lax.axis_size("req")
    devices_all = group_count * group_width
    group_index = lax.axis_index("req")
    member_index = lax.axis_index("exp")
    slots_here, local_rows, model_width = hidden.shape
    head_count = q_new.shape[1]
    head_dim = q_new.shape[3]
    experts_all = router.shape[1]
    pair_count = slots_here * head_count
    pairs_here = pair_count // group_width
    members_of_slot = head_count // pairs_here

    requests = lax.dynamic_slice_in_dim(slot_request, group_index * slots_here, slots_here)
    fresh_sel = from_holders(jnp.stack([q_new, k_new, v_new], 1), slot_request, requests)
    fresh_out = (
        fresh_sel.reshape(
            slots_here, 3, members_of_slot, pairs_here, local_rows, head_dim
        )
        .transpose(0, 2, 1, 3, 4, 5)
        .reshape(group_width, 3, pairs_here, local_rows, head_dim)
    )
    fresh = lax.all_to_all(fresh_out, "exp", split_axis=0, concat_axis=0, tiled=True)
    slot_here = group_index * slots_here + member_index // members_of_slot
    length = lax.dynamic_index_in_dim(lengths, slot_here, keepdims=False)

    hidden_sel = jnp.take(lax.all_gather(hidden, "req", axis=0, tiled=True), requests, axis=0)
    route_group = lax.all_gather(routes, ("req", "exp"), axis=0).reshape(
        group_count, group_width, slots_here, local_rows, -1
    )
    route_group = route_group.transpose(0, 2, 1, 3, 4).reshape(
        group_count * slots_here, group_width, local_rows, -1
    )
    route_group = jnp.take(route_group, requests, axis=0)

    context, cycle_out = attend(fresh, cycle_cache, sink_cache, length)
    context_rows = lax.all_to_all(context, "exp", split_axis=0, concat_axis=0, tiled=True)
    context_rows = context_rows.reshape(slots_here, head_count, local_rows, head_dim)
    projected = jnp.einsum(
        "shqd,hde->sqe",
        context_rows,
        w_out.reshape(head_count, head_dim, model_width),
        preferred_element_type=jnp.float32,
    )
    residual = hidden_sel.astype(jnp.float32) + projected
    inverse = lax.rsqrt(jnp.mean(residual * residual, axis=-1, keepdims=True) + 1e-06)
    normed = (residual * inverse * norm_gain).astype(jnp.bfloat16)

    most_slots = max(2, local_rows // 8)
    sub_here = experts_all * SPLIT // devices_all
    units = max(1, sub_here // SPLIT)
    pieces = max(1, SPLIT // sub_here)
    partners = group_index ^ jnp.arange(group_count, dtype=jnp.int32)
    owners = partners * group_width + member_index
    served = (
        owners[:, None] * units + jnp.arange(units, dtype=jnp.int32)[None, :]
    ).reshape(-1) // pieces
    served_count = group_count * units
    hidden_units = w_gate.shape[1] // units
    earlier_rows = jnp.arange(local_rows)[:, None] > jnp.arange(local_rows)[None, :]

    gathered, landed, kept, moe = [], [], [], []
    for slot in range(slots_here):
        rows_group = lax.all_gather(normed[slot], "exp", axis=0)
        gathered.append(rows_group)
        named = jnp.any(route_group[slot][..., None] == served, axis=2)
        earlier = jnp.einsum(
            "qp,bpe->bqe",
            earlier_rows.astype(jnp.bfloat16),
            named.astype(jnp.bfloat16),
            preferred_element_type=jnp.float32,
        ).astype(jnp.int32)
        chosen = named[..., None] & (
            earlier[..., None] == jnp.arange(most_slots, dtype=jnp.int32)
        )
        kept.append(chosen)
        outgoing = jnp.einsum(
            "bqer,bqd->ebrd",
            chosen.astype(jnp.bfloat16),
            rows_group,
            preferred_element_type=jnp.float32,
        ).astype(jnp.bfloat16)
        landed.append(
            swap_all(outgoing.reshape(group_count, units, group_width * most_slots, model_width))
        )
    for slot in range(slots_here):
        replies = []
        for unit in range(units):
            rows = jnp.concatenate([part[unit] for part in landed[slot]], 0)
            span = slice(unit * hidden_units, (unit + 1) * hidden_units)
            gate_part = jnp.dot(rows, w_gate[:, span], preferred_element_type=jnp.float32)
            up_part = jnp.dot(rows, w_up[:, span], preferred_element_type=jnp.float32)
            active = (jax.nn.silu(gate_part) * up_part).astype(jnp.bfloat16)
            reply = jnp.dot(active, w_down[span], preferred_element_type=jnp.float32)
            replies.append(
                reply.astype(jnp.bfloat16).reshape(
                    group_count, group_width * most_slots, model_width
                )
            )
        back = swap_all(
            [jnp.stack([reply[k] for reply in replies]) for k in range(group_count)]
        )
        returned = jnp.concatenate(back, 0).reshape(
            served_count, group_width, most_slots, model_width
        )

        logits = jnp.einsum(
            "bqd,de->bqe", gathered[slot], router, preferred_element_type=jnp.float32
        )
        routed = jnp.any(
            route_group[slot][..., None] == jnp.arange(experts_all, dtype=jnp.int32), axis=2
        )
        gates_all = jax.nn.softmax(jnp.where(routed, logits, -jnp.inf), axis=-1)
        gates = jnp.take(gates_all, served, axis=2)
        weights = jnp.where(kept[slot], gates[..., None], 0.0)
        weights_high = lax.reduce_precision(weights, 8, 7)
        weights_low = (weights - weights_high).astype(jnp.bfloat16)
        weights_high = weights_high.astype(jnp.bfloat16)

        def combined(part):
            return jnp.einsum(
                "bqer,ebrd->bqd", part, returned, preferred_element_type=jnp.float32
            )

        partial = (combined(weights_high) + combined(weights_low)).astype(jnp.bfloat16)
        moe.append(lax.psum_scatter(partial, "exp", scatter_dimension=0, tiled=False))
    layer_out = (residual + jnp.stack(moe).astype(jnp.float32)).astype(jnp.bfloat16)
    return (layer_out, cycle_out)


def solution(mesh):
    in_specs = (
        P("req", "exp", None),
        P("req", None, "exp", None),
        P("req", None, "exp", None),
        P("req", None, "exp", None),
        P("req", "exp", None),
        P(),
        P(),
        P(("req", "exp"), None, None, None),
        P(("req", "exp"), None, None, None),
        P(),
        P(),
        P(),
        P(None, ("req", "exp")),
        P(None, ("req", "exp")),
        P(("req", "exp"), None),
    )
    out_specs = (P("req", "exp", None), P(("req", "exp"), None, None, None))
    return jax.shard_map(
        on_device, mesh=mesh, in_specs=in_specs, out_specs=out_specs, check_vma=False
    )
```
